256 devices in a mesh: dp: 16 (over x, y), seq: 16 (over z, core).
Axes of the slice: x: 4, y: 4, z: 8, core: 2. Of those that a mesh axis runs over, the one named last changes fastest.
Arguments:
- queries: bfloat16 [32768, 40, 128], P(('dp', 'seq')), parts along dimension 0, may hold values from -100 to 100
- keys: bfloat16 [32768, 8, 128], P(('dp', 'seq')), parts along dimension 0, may hold values from -4 to 4
- values: bfloat16 [32768, 8, 128], P(('dp', 'seq')), parts along dimension 0, may hold values from -40 to 40
- grad_out: bfloat16 [32768, 40, 128], P(('dp', 'seq')), parts along dimension 0, may hold values from -6 to 6
- doc_ids: int32 [32768], P(('dp', 'seq')), parts along dimension 0, may hold values from 0 to 5, never falling along the last dimension, each value on 1 to 1024 neighbouring positions
Outputs:
- attended: bfloat16 [32768, 40, 128], P(('dp', 'seq')), parts along dimension 0
- grad_queries: bfloat16 [32768, 40, 128], P(('dp', 'seq')), parts along dimension 0
- grad_keys: bfloat16 [32768, 8, 128], P(('dp', 'seq')), parts along dimension 0
- grad_values: bfloat16 [32768, 8, 128], P(('dp', 'seq')), parts along dimension 0
The draws below stay inside these ranges and needn't reach their ends.
There are 16 independent parts, one for each index of `dp`. The reference program is written for one: setup_inputs(seed, part) draws one part's arguments, and reference() takes and returns one part's arrays. A program takes and returns all parts, laid end to end along the dimension named above; each array names one. Nothing has to cross between parts.
Inputs may be any that keep to these rules, and one draw needn't show every extreme that they name: `doc_ids`: document numbers never fall along the sequence, so each document is one contiguous run; the longest runs exactly half of the 2048 positions.
All inputs are finite; a program needn't handle non-finite values.
Results may differ from the reference program's by a relative error of at most 0.04.
Values may be sent and summed in bfloat16 or wider, within the bound.
A program may use at most 192 MiB of HBM per device.

```python
import math
import jax
import jax.numpy as jnp
import numpy as np
from jax import lax

QH = 40
KVH = 8
HD = 128
DOCS = 6
SEQ = 2048


def shared_keys(key):
    base = jnp.clip(jax.random.normal(jax.random.fold_in(key, 101), (SEQ, KVH, HD), jnp.float32), -4.0, 4.0)
    marks = jax.random.randint(jax.random.fold_in(key, 102), (SEQ,), 0, 64) == 0
    marks = marks & (jnp.arange(SEQ) >= 2)
    keys_out = base
    strength = 12.0 + 6.0 * jax.random.randint(jax.random.fold_in(key, 103), (SEQ,), 0, 3).astype(jnp.float32)
    return (keys_out, marks, strength)


def draw_queries(key, part):
    lift = 0.0
    keys_out, marks, strength = shared_keys(key)
    key = jax.random.fold_in(key, 1)
    base = jnp.clip(jax.random.normal(key, (SEQ, QH, HD), jnp.float32), -4.0, 4.0)
    before = jnp.concatenate([keys_out[:1], keys_out[:-1]], axis=0)
    spiked = jnp.repeat(before, QH // KVH, axis=1) * strength[:, None, None]
    chosen = marks & (lift > 0.5)
    return jnp.where(chosen[:, None, None], spiked, base).astype(jnp.bfloat16)


def draw_keys(key, part):
    keys_out, marks, strength = shared_keys(key)
    return keys_out.astype(jnp.bfloat16)


def draw_values(key, part):
    key = jax.random.fold_in(key, 3)
    base = jnp.clip(jax.random.normal(key, (SEQ, KVH, HD), jnp.float32), -4.0, 4.0)
    return base.astype(jnp.bfloat16)


def block_scale(own_key, dims, split, low, high):
    level = 1.0
    for position, shards_of in split:
        draws = jax.random.uniform(jax.random.fold_in(jax.random.fold_in(own_key, 6), position), (shards_of,), jnp.float32, low / len(split), high / len(split))
        level = level * jnp.repeat(jnp.exp(draws), dims[position] // shards_of).reshape((-1,) + (1,) * (len(dims) - 1 - position))
    return level


def profile(number_of, total, reach, lean):
    loads = [(1 << 20) // math.isqrt(grade ** lean) + 1 for grade in range(2, number_of + 1)]
    spare, given = total - reach - (number_of - 1), [1] * (number_of - 1)
    while spare > 0:
        free = [i for i in range(number_of - 1) if given[i] < reach]
        pool, budget = sum([loads[i] for i in free]), spare
        for i in free:
            extra = min(reach - given[i], max(1, budget * loads[i] // pool), spare)
            given[i] = given[i] + extra
            spare = spare - extra
    return np.array([reach] + given)


def ragged(key, count, total, limit, slope):
    if count == 2:
        one = jax.random.randint(key, (), max(1, total - limit), min(limit, total - 1) + 1)
        return jnp.stack([one, total - one])
    sizes = jnp.asarray(profile(count, total, limit, slope), jnp.int32)
    twos = (count - 1) // 2
    donor, receiver = sizes[1:1 + 2 * twos:2], sizes[2:2 + 2 * twos:2]
    room = jnp.minimum(donor - 1, limit - receiver)
    moved = jax.random.randint(jax.random.fold_in(key, 1), (twos,), 0, 1 << 20) % (room + 1)
    sizes = sizes.at[1:1 + 2 * twos:2].set(donor - moved).at[2:2 + 2 * twos:2].set(receiver + moved)
    return sizes[jax.random.permutation(jax.random.fold_in(key, 2), count)]


def noise(stream_key, extent, scale, limit, pieces=(), kind=jnp.bfloat16):
    entries = scale * jax.random.normal(stream_key, extent, jnp.float32)
    if pieces:
        entries = entries * block_scale(stream_key, extent, pieces, -0.22, 0.18)
    return jnp.clip(entries, -limit, limit).astype(kind)


def setup_inputs(seed: int = 0, part: int = 0) -> dict:
    streams_of = jax.random.split(jax.random.key(seed), 6)
    own_keys = jax.random.split(jax.random.fold_in(streams_of[5], part), 6)
    return {
        "queries": draw_queries(jax.random.fold_in(jax.random.fold_in(streams_of[5], part), 71), part),
        "keys": draw_keys(jax.random.fold_in(jax.random.fold_in(streams_of[5], part), 71), part),
        "values": draw_values(jax.random.fold_in(jax.random.fold_in(streams_of[5], part), 71), part),
        "grad_out": noise(own_keys[3], (SEQ, QH, HD), 1.0, 6.0, ((0, 16),)),
        "doc_ids": jnp.searchsorted(jnp.cumsum(ragged(own_keys[4], DOCS, SEQ, SEQ // 2, 0)), jnp.arange(SEQ), side="right").astype(jnp.int32),
    }


def head_pass(q_head, k_head, v_head, g_head, allowed):
    score_scale = 1.0 / math.sqrt(HD)
    scores = jnp.dot(q_head, k_head.T, preferred_element_type=jnp.float32) * score_scale
    scores = jnp.where(allowed, scores, -jnp.inf)
    row_max = lax.optimization_barrier(jnp.max(scores, axis=-1, keepdims=True))
    raised = jnp.exp(scores - row_max)
    probs = raised / lax.optimization_barrier(jnp.sum(raised, axis=-1, keepdims=True))
    probs_low = probs.astype(jnp.bfloat16)
    attended = jnp.dot(probs_low, v_head, preferred_element_type=jnp.float32).astype(jnp.bfloat16)
    row_delta = lax.optimization_barrier(jnp.sum(g_head.astype(jnp.float32) * attended.astype(jnp.float32), axis=-1))
    grad_prob = jnp.dot(g_head, v_head.T, preferred_element_type=jnp.float32)
    grad_score_low = (probs * (grad_prob - row_delta[:, None])).astype(jnp.bfloat16)
    grad_query = (jnp.dot(grad_score_low, k_head, preferred_element_type=jnp.float32) * score_scale).astype(jnp.bfloat16)
    key_part = jnp.dot(grad_score_low.T, q_head, preferred_element_type=jnp.float32) * score_scale
    value_part = jnp.dot(probs_low.T, g_head, preferred_element_type=jnp.float32)
    return (attended, grad_query, key_part, value_part)

def reference(queries, keys, values, grad_out, doc_ids):
    group_size = QH // KVH
    positions = jnp.arange(SEQ, dtype=jnp.int32)
    allowed = (doc_ids[:, None] == doc_ids[None, :]) & (positions[None, :] <= positions[:, None])

    def per_group(group_idx):
        q_group = lax.dynamic_slice_in_dim(queries, (group_idx * group_size).astype(jnp.int32), group_size, 1)
        g_group = lax.dynamic_slice_in_dim(grad_out, (group_idx * group_size).astype(jnp.int32), group_size, 1)
        k_head = lax.dynamic_index_in_dim(keys, group_idx, 1, keepdims=False)
        v_head = lax.dynamic_index_in_dim(values, group_idx, 1, keepdims=False)
        out_list = []
        dq_list = []
        key_sum = jnp.zeros((SEQ, keys.shape[2]), jnp.float32)
        value_sum = jnp.zeros((SEQ, keys.shape[2]), jnp.float32)
        for member in range(group_size):
            result = head_pass(q_group[:, member], k_head, v_head, g_group[:, member], allowed)
            out_list.append(result[0])
            dq_list.append(result[1])
            key_sum = key_sum + result[2]
            value_sum = value_sum + result[3]
        return (jnp.stack(out_list, 1), jnp.stack(dq_list, 1), key_sum, value_sum)
    out_all, dq_all, key_all, value_all = lax.map(per_group, jnp.arange(KVH, dtype=jnp.int32))
    attended = jnp.transpose(out_all, (1, 0, 2, 3)).reshape(SEQ, QH, queries.shape[2])
    grad_queries = jnp.transpose(dq_all, (1, 0, 2, 3)).reshape(SEQ, QH, queries.shape[2])
    grad_keys = jnp.transpose(key_all, (1, 0, 2)).astype(jnp.bfloat16)
    grad_values = jnp.transpose(value_all, (1, 0, 2)).astype(jnp.bfloat16)
    return (attended, grad_queries, grad_keys, grad_values)
```

```python
import functools
import math

import jax
import jax.numpy as jnp
from jax import lax
from jax.experimental import pallas as pl
from jax.experimental.pallas import tpu as pltpu
from jax.sharding import PartitionSpec as P

MESH = pl.DeviceIdType.MESH
COMPUTE = True
COMM = True
BACK = 4
LINE = BACK + 1
DOC_VALUES = 6


def rows_at(distance, rows):
    return pl.ds(pl.multiple_of((2 * BACK - distance) * rows, rows), rows)


def kernel(
    q_ref, g_ref, kv_ref, doc_ref, o_ref, dq_ref, dkv_ref,
    kv_all, doc_all, part_own, part_sib, sib_got, sums, sums_got,
    s_ref, p_ref, ds_ref, qt_ref, gt_ref, qs_ref, gs_ref, kt_ref, vt_ref,
    start_ref, delta_ref, inv_ref,
    kv_up_recv, kv_sib_recv, doc_up_recv, doc_sib_recv, sib_recv, sums_recv,
    send_sems,
):
    units, rows, head = kv_ref.shape
    groups = units // 2
    cols = q_ref.shape[1]
    members = cols // rows
    window = kv_all.shape[1]
    blocks = window // rows
    size = lax.axis_size("seq")
    me = lax.axis_index("seq")
    core = lax.rem(me, 2)
    up = lax.rem(me + 2, size)
    down = lax.rem(me + size - 2, size)
    sib = me + 1 - 2 * core
    scale = 1.0 / math.sqrt(head)
    log_scale = scale * math.log2(math.e)
    f32, bf16 = jnp.float32, jnp.bfloat16

    own = pl.ds(window - rows, rows)
    kv_all[:, own, :] = kv_ref[...]
    doc_all[64:72, :] = doc_ref[...]
    sib_got[:, 0] = jnp.zeros((units, rows, head), bf16)
    sib_got[:, BACK] = jnp.zeros((units, rows, head), bf16)

    def remote(src, dst, send, recv, to):
        return pltpu.make_async_remote_copy(
            src_ref=src, dst_ref=dst, send_sem=send_sems.at[send], recv_sem=recv,
            device_id={"seq": to}, device_id_type=MESH,
        )

    def kv_up(unit, k):
        return remote(
            kv_all.at[unit, rows_at(2 * k, rows)], kv_all.at[unit, rows_at(2 * k + 2, rows)],
            0, kv_up_recv.at[unit, k], up,
        )

    def kv_share(unit, k):
        slot = k - core
        return remote(
            kv_all.at[unit, rows_at(2 * k, rows)], kv_all.at[unit, rows_at(2 * slot + 1, rows)],
            1, kv_sib_recv.at[unit, slot], sib,
        )

    def doc_up(k):
        return remote(
            doc_all.at[rows_at(2 * k, 8)], doc_all.at[rows_at(2 * k + 2, 8)],
            2, doc_up_recv.at[k], up,
        )

    def doc_share(k):
        slot = k - core
        return remote(
            doc_all.at[rows_at(2 * k, 8)], doc_all.at[rows_at(2 * slot + 1, 8)],
            3, doc_sib_recv.at[slot], sib,
        )

    def part_share(unit):
        return remote(
            part_sib.at[unit], sib_got.at[unit, pl.ds(1 - core, BACK)],
            4, sib_recv.at[unit], sib,
        )

    def sum_down(unit, j):
        return remote(
            sums.at[unit, j - 1], sums_got.at[unit, j - 1],
            5, sums_recv.at[unit, j - 1], down,
        )

    barrier = pltpu.get_barrier_semaphore()
    for other in (up, down, sib):
        pl.semaphore_signal(barrier, inc=1, device_id={"seq": other}, device_id_type=MESH)
    pl.semaphore_wait(barrier, 3)

    def kv_event(step, k):
        unit = step - k

        @pl.when((unit >= 0) & (unit < units))
        def _():
            if k > 0:
                @pl.when(unit == 0)
                def _():
                    doc_up(k - 1).wait_recv()
                kv_up(unit, k - 1).wait_recv()
            if k < BACK:
                @pl.when(unit == 0)
                def _():
                    doc_up(k).start()
                kv_up(unit, k).start()

            def share():
                @pl.when(unit == 0)
                def _():
                    doc_share(k).start()
                kv_share(unit, k).start()

            if k == 0:
                pl.when(core == 0)(share)
            elif k == BACK:
                pl.when(core == 1)(share)
            else:
                share()

    def sum_event(step, j):
        unit = step - 2 * BACK + 1 - (BACK - j)

        @pl.when((unit >= 0) & (unit < units))
        def _():
            if j == BACK:
                part_share(unit).wait_recv()
            total = part_own[unit, j] + sib_got[unit, j].astype(f32)
            if j < BACK:
                sum_down(unit, j + 1).wait_recv()
                total = total + sums_got[unit, j].astype(f32)
            if j > 0:
                sums[unit, j - 1] = total.astype(bf16)
                sum_down(unit, j).start()
            else:
                factor = jnp.where(unit % 2 == 1, scale, 1.0).astype(f32)
                dkv_ref[unit] = (total * factor).astype(bf16)

    def find_starts():
        docs = doc_ref[0:1, :]
        old = lax.broadcasted_iota(jnp.int32, (8 * blocks, rows), 0) // 8
        old = old + (me - 2 * BACK) < 0
        all_docs = jnp.where(old, -1, doc_all[...])
        start = jnp.zeros((1, rows), jnp.int32)
        for value in range(DOC_VALUES):
            less = jnp.where(all_docs < value, 1, 0)
            count = jnp.sum(jnp.sum(less, axis=0, keepdims=True), axis=1, keepdims=True) // 8
            start = jnp.where(docs == value, count, start)
        for member in range(members):
            start_ref[:, member * rows : (member + 1) * rows] = start

    def forward(group, first, width):
        at = slice(first, first + width)
        qt = q_ref[group, at, :].T
        qt_ref[:, at] = qt
        start = start_ref[:, at]
        top = jnp.full((8, width), -jnp.inf, f32)
        for block in range(blocks):
            span = slice(block * rows, (block + 1) * rows)
            s = jnp.dot(kv_all[2 * group, span, :], qt, preferred_element_type=f32)
            where = block * rows + lax.broadcasted_iota(jnp.int32, (rows, width), 0)
            allowed = where >= start
            if block == blocks - 1:
                mine = lax.broadcasted_iota(jnp.int32, (rows, width), 1) % rows
                allowed = allowed & (where - block * rows <= mine)
            s = jnp.where(allowed, s, -jnp.inf)
            s_ref[span, at] = s
            top = jnp.maximum(top, jnp.max(s.reshape(rows // 8, 8, width), axis=0))
        top = jnp.max(top, axis=0, keepdims=True)
        total = jnp.zeros((8, width), f32)
        for block in range(blocks):
            span = slice(block * rows, (block + 1) * rows)
            p = jnp.exp2((s_ref[span, at] - top) * log_scale)
            total = total + jnp.sum(p.reshape(rows // 8, 8, width), axis=0)
            p_ref[span, at] = p.astype(bf16)
        inv = 1.0 / jnp.sum(total, axis=0, keepdims=True)
        inv_ref[:, at] = inv
        ot = jnp.dot(vt_ref[...], p_ref[:, at], preferred_element_type=f32) * inv
        ot = ot.astype(bf16)
        o_ref[group, at, :] = ot.T
        gt = g_ref[group, at, :].T
        gt_ref[:, at] = gt
        delta_ref[:, at] = jnp.sum(gt.astype(f32) * ot.astype(f32), axis=0, keepdims=True)
        gs_ref[:, at] = (gt.astype(f32) * inv).astype(bf16)
        qs_ref[:, at] = (qt.astype(f32) * inv).astype(bf16)

    def backward(group, first, width):
        at = slice(first, first + width)
        gt = gt_ref[:, at]
        delta = delta_ref[:, at]
        for block in range(blocks):
            span = slice(block * rows, (block + 1) * rows)
            dp = jnp.dot(kv_all[2 * group + 1, span, :], gt, preferred_element_type=f32)
            ds_ref[span, at] = (p_ref[span, at].astype(f32) * (dp - delta)).astype(bf16)
        dqt = jnp.dot(kt_ref[...], ds_ref[:, at], preferred_element_type=f32)
        dq_ref[group, at, :] = (dqt * (inv_ref[:, at] * scale)).astype(bf16).T

    def to_keys(unit, left, right):
        for block in range(blocks):
            span = slice(block * rows, (block + 1) * rows)
            part = lax.dot_general(
                left[span, :], right[...], (((1,), (1,)), ((), ())), preferred_element_type=f32
            )
            distance = blocks - 1 - block
            if distance % 2 == 0:
                part_own[unit, distance // 2] = part
            else:
                part_sib[unit, distance // 2] = part.astype(bf16)

    chunks = []
    for first in range(0, cols, 2 * rows):
        chunks.append((first, min(2 * rows, cols - first)))
    lag = BACK - 1

    def half(step, which, group):
        run = (group >= 0) & (group < groups) & COMPUTE
        unit = 2 * group + which
        last = len(chunks)
        kv_event(step, 0)

        @pl.when((group >= 0) & (group < groups))
        def _():
            @pl.when(unit == 0)
            def _():
                for slot in range(BACK):
                    doc_share(core + slot).wait_recv()
            if which == 0:
                for slot in range(BACK):
                    kv_share(unit, core + slot).wait_recv()
                for slot in range(BACK):
                    kv_share(unit + 1, core + slot).wait_recv()

        @pl.when(run)
        def _():
            if which == 0:
                pl.when(group == 0)(find_starts)
                kt_ref[...] = kv_all[2 * group].T
            else:
                pass

        for piece in range(last + 1):
            kv_event(step, piece + 1)
            sum_event(step, BACK - piece)

            @pl.when(run)
            def _():
                if which == 0:
                    if piece < last:
                        if piece == 0:
                            vt_ref[...] = kv_all[2 * group + 1].T
                        forward(group, *chunks[piece])
                    else:
                        to_keys(unit, p_ref, gs_ref)
                else:
                    if piece < last:
                        backward(group, *chunks[piece])
                    else:
                        to_keys(unit, ds_ref, qs_ref)
        sum_event(step, 0)

        @pl.when((group >= 0) & (group < groups))
        def _():
            part_share(unit).start()

    def body(turn, carry):
        half(2 * turn, 0, turn - lag)
        half(2 * turn + 1, 1, turn - lag)
        return carry

    turns = groups + lag + BACK - 1
    lax.fori_loop(0, turns, body, 0)

    def drain(ref, index):
        pltpu.make_async_copy(ref, ref, send_sems.at[index]).wait()

    moved = pl.ds(rows, BACK * rows)
    drain(kv_all.at[:, moved], 0)
    drain(kv_all.at[:, moved], 1)
    drain(doc_all.at[pl.ds(0, 8 * BACK)], 2)
    drain(doc_all.at[pl.ds(0, 8 * BACK)], 3)
    drain(part_sib, 4)
    drain(sums, 5)


def shards(queries, keys, values, grad_out, doc_ids):
    rows, heads, head = queries.shape
    groups = keys.shape[1]
    members = heads // groups
    units = 2 * groups
    cols = members * rows
    blocks = 2 * BACK + 1
    window = blocks * rows
    f32, bf16 = jnp.float32, jnp.bfloat16

    def by_group(array):
        return jnp.transpose(array, (1, 0, 2)).reshape(groups, cols, head)

    def by_row(array):
        return jnp.transpose(array.reshape(heads, rows, head), (1, 0, 2))

    pairs = jnp.stack([keys, values], axis=2)
    kv = jnp.transpose(pairs, (1, 2, 0, 3)).reshape(units, rows, head)
    docs = jnp.broadcast_to(doc_ids[None, :], (8, rows))
    vmem = pl.BlockSpec(memory_space=pltpu.VMEM)
    DMA = pltpu.SemaphoreType.DMA
    big = jax.ShapeDtypeStruct((groups, cols, head), bf16)
    out, dq, dkv = pl.pallas_call(
        kernel,
        out_shape=(big, big, jax.ShapeDtypeStruct((units, rows, head), bf16)),
        in_specs=[vmem] * 4,
        out_specs=[vmem] * 3,
        scratch_shapes=[
            pltpu.VMEM((units, window, head), bf16),
            pltpu.VMEM((8 * blocks, rows), jnp.int32),
            pltpu.VMEM((units, LINE, rows, head), f32),
            pltpu.VMEM((units, BACK, rows, head), bf16),
            pltpu.VMEM((units, LINE, rows, head), bf16),
            pltpu.VMEM((units, BACK, rows, head), bf16),
            pltpu.VMEM((units, BACK, rows, head), bf16),
            pltpu.VMEM((window, cols), f32),
            pltpu.VMEM((window, cols), bf16),
            pltpu.VMEM((window, cols), bf16),
            pltpu.VMEM((head, cols), bf16),
            pltpu.VMEM((head, cols), bf16),
            pltpu.VMEM((head, cols), bf16),
            pltpu.VMEM((head, cols), bf16),
            pltpu.VMEM((head, window), bf16),
            pltpu.VMEM((head, window), bf16),
            pltpu.VMEM((1, cols), jnp.int32),
            pltpu.VMEM((1, cols), f32),
            pltpu.VMEM((1, cols), f32),
            DMA((units, BACK)),
            DMA((units, BACK)),
            DMA((BACK,)),
            DMA((BACK,)),
            DMA((units,)),
            DMA((units, BACK)),
            DMA((6,)),
        ],
        compiler_params=pltpu.CompilerParams(
            collective_id=0, has_side_effects=True, vmem_limit_bytes=60 * 1024 * 1024
        ),
        name="ring_attention",
    )(by_group(queries), by_group(grad_out), kv, docs)
    dkv = jnp.transpose(dkv.reshape(groups, 2, rows, head), (1, 2, 0, 3))
    return (by_row(out), by_row(dq), dkv[1], dkv[0])


def solution(mesh):
    spec = P(("dp", "seq"), None, None)
    return jax.shard_map(
        shards,
        mesh=mesh,
        in_specs=(spec, spec, spec, spec, P(("dp", "seq"))),
        out_specs=(spec, spec, spec, spec),
        check_vma=False,
    )
```

```python
import functools
import math

import jax
import jax.numpy as jnp
from jax import lax
from jax.experimental import pallas as pl
from jax.experimental.pallas import tpu as pltpu
from jax.sharding import PartitionSpec as P

MESH = pl.DeviceIdType.MESH
BACK = 4
LINE = BACK + 1
PIECES = 4
SPANS = 3
KV_AT = (0, 4, 9, 14, 19)
SUM_AT = (22, 17, 12, 7, 2)
FIRST = 6
DOC_VALUES = 6


def rows_at(distance, rows):
    return pl.ds(pl.multiple_of((2 * BACK - distance) * rows, rows), rows)


def kernel(
    q_hbm, g_hbm, k_hbm, v_hbm, doc_hbm, o_hbm, dq_hbm, dk_hbm, dv_hbm,
    q16, g16, k16, v16, doc_row, q32, g32, k32, v32, qt_all, gt_all,
    kv_all, doc_all, part_own, part_sib, sib_got, sums, sums_got,
    s_ref, dp_ref, p_ref, ds_ref, qs_ref, gs_ref, kt_ref, vt_ref,
    start_ref, top_ref, delta_ref, inv_ref,
    kv_up_recv, kv_sib_recv, doc_up_recv, doc_sib_recv, sib_recv, sums_recv,
    send_sems, local_sems,
):
    units, window, head = kv_all.shape
    rows = doc_row.shape[1]
    groups = units // 2
    cols = s_ref.shape[1]
    members = cols // rows
    heads = members * groups
    blocks = window // rows
    size = lax.axis_size("seq")
    me = lax.axis_index("seq")
    core = lax.rem(me, 2)
    up = lax.rem(me + 2, size)
    down = lax.rem(me + size - 2, size)
    sib = me + 1 - 2 * core
    scale = 1.0 / math.sqrt(head)
    log_scale = scale * math.log2(math.e)
    f32, bf16 = jnp.float32, jnp.bfloat16

    barrier = pltpu.get_barrier_semaphore()
    for other in (up, down, sib):
        pl.semaphore_signal(barrier, inc=1, device_id={"seq": other}, device_id_type=MESH)

    loads = [
        pltpu.make_async_copy(src, dst, local_sems.at[index])
        for index, (src, dst) in enumerate(
            ((k_hbm, k16), (v_hbm, v16), (doc_hbm, doc_row), (q_hbm, q16), (g_hbm, g16))
        )
    ]
    for load in loads:
        load.start()
    sib_got[:, 0] = jnp.zeros((units, rows, head), bf16)
    sib_got[:, BACK] = jnp.zeros((units, rows, head), bf16)
    for load in loads[:3]:
        load.wait()
    k32[...] = k16[...].astype(f32)
    v32[...] = v16[...].astype(f32)
    own = slice(window - rows, window)
    for group in range(groups):
        kv_all[2 * group, own, :] = k32[pl.ds(group, rows, stride=groups), :].astype(bf16)
        kv_all[2 * group + 1, own, :] = v32[pl.ds(group, rows, stride=groups), :].astype(bf16)
    doc_all[16 * BACK : 16 * BACK + 8, :] = jnp.broadcast_to(doc_row[...], (8, rows))
    pl.semaphore_wait(barrier, 3)

    def remote(src, dst, send, recv, to):
        return pltpu.make_async_remote_copy(
            src_ref=src, dst_ref=dst, send_sem=send_sems.at[send], recv_sem=recv,
            device_id={"seq": to}, device_id_type=MESH,
        )

    def kv_up(unit, k):
        return remote(
            kv_all.at[unit, rows_at(2 * k, rows)], kv_all.at[unit, rows_at(2 * k + 2, rows)],
            0, kv_up_recv.at[unit, k], up,
        )

    def kv_share(unit, k):
        slot = k - core
        return remote(
            kv_all.at[unit, rows_at(2 * k, rows)], kv_all.at[unit, rows_at(2 * slot + 1, rows)],
            1, kv_sib_recv.at[unit, slot], sib,
        )

    def doc_up(k):
        return remote(
            doc_all.at[rows_at(2 * k, 8)], doc_all.at[rows_at(2 * k + 2, 8)],
            2, doc_up_recv.at[k], up,
        )

    def doc_share(k):
        slot = k - core
        return remote(
            doc_all.at[rows_at(2 * k, 8)], doc_all.at[rows_at(2 * slot + 1, 8)],
            3, doc_sib_recv.at[slot], sib,
        )

    def part_share(unit):
        return remote(
            part_sib.at[unit], sib_got.at[unit, pl.ds(1 - core, BACK)],
            4, sib_recv.at[unit], sib,
        )

    def sum_down(unit, j):
        return remote(
            sums.at[unit, j - 1], sums_got.at[unit, j - 1],
            5, sums_recv.at[unit, j - 1], down,
        )

    def kv_event(step, k):
        unit = step - KV_AT[k] // PIECES

        @pl.when((unit >= 0) & (unit < units))
        def _():
            if k > 0:
                @pl.when(unit == 0)
                def _():
                    doc_up(k - 1).wait_recv()
                kv_up(unit, k - 1).wait_recv()
            if k < BACK:
                @pl.when(unit == 0)
                def _():
                    doc_up(k).start()
                kv_up(unit, k).start()

            def share():
                @pl.when(unit == 0)
                def _():
                    doc_share(k).start()
                kv_share(unit, k).start()

            if k == 0:
                pl.when(core == 0)(share)
            elif k == BACK:
                pl.when(core == 1)(share)
            else:
                share()

    def sum_event(step, which, j):
        back = FIRST + 1 + SUM_AT[j] // PIECES
        unit = step - back

        @pl.when((unit >= 0) & (unit < units))
        def _():
            if j == BACK:
                part_share(unit).wait_recv()
            total = part_own[unit, j] + sib_got[unit, j].astype(f32)
            if j < BACK:
                sum_down(unit, j + 1).wait_recv()
                total = total + sums_got[unit, j].astype(f32)
            if j > 0:
                sums[unit, j - 1] = total.astype(bf16)
                sum_down(unit, j).start()
            elif (which - back) % 2 == 1:
                k32[pl.ds(unit // 2, rows, stride=groups), :] = total * scale
            else:
                v32[pl.ds(unit // 2, rows, stride=groups), :] = total

    def find_starts():
        docs = doc_row[...]
        old = lax.broadcasted_iota(jnp.int32, (8 * blocks, rows), 0) // 8
        old = old + (me - 2 * BACK) < 0
        all_docs = jnp.where(old, -1, doc_all[...])
        start = jnp.zeros((1, rows), jnp.int32)
        for value in range(DOC_VALUES):
            less = jnp.where(all_docs < value, 1, 0)
            count = jnp.sum(jnp.sum(less, axis=0, keepdims=True), axis=1, keepdims=True) // 8
            start = jnp.where(docs == value, count, start)
        for member in range(members):
            start_ref[:, member * rows : (member + 1) * rows] = start

    def widen(source, dest):
        def move(index, carry):
            at = pl.ds(pl.multiple_of(index * 256, 256), 256)
            dest[at, :] = source[at, :].astype(dest.dtype)
            return carry

        lax.fori_loop(0, source.shape[0] // 256, move, 0)

    def by_row(source, dest):
        def move(index, carry):
            pair = [
                source[pl.ds(2 * index + odd, heads, stride=rows), :] for odd in (0, 1)
            ]
            at = pl.ds(pl.multiple_of(2 * heads * index, 2 * heads), 2 * heads)
            dest[at, :] = jnp.concatenate(pair, axis=0).astype(dest.dtype)
            return carry

        lax.fori_loop(0, rows // 2, move, 0)

    def prepare(number):
        for index in (2 * number, 2 * number + 1):
            every = pl.ds(index, rows, stride=heads)
            qt_all[index] = q32[every, :].T.astype(bf16)
            gt_all[index] = g32[every, :].T.astype(bf16)

    def pick(ref, group):
        return jnp.concatenate([ref[group * members + index] for index in range(members)], axis=1)

    def put(ref, group, value):
        for index in range(members):
            at = pl.ds(pl.multiple_of((group * members + index) * rows, rows), rows)
            ref[at, :] = value[:, index * rows : (index + 1) * rows].T

    def score(group):
        start = start_ref[...]
        s_ref[...] = jnp.dot(kv_all[2 * group], pick(qt_all, group), preferred_element_type=f32)
        top = jnp.full((8, cols), -jnp.inf, f32)
        for block in range(blocks):
            span = slice(block * rows, (block + 1) * rows)
            where = block * rows + lax.broadcasted_iota(jnp.int32, (rows, cols), 0)
            allowed = where >= start
            if block == blocks - 1:
                mine = lax.broadcasted_iota(jnp.int32, (rows, cols), 1) % rows
                allowed = allowed & (where - block * rows <= mine)
            s = jnp.where(allowed, s_ref[span], -jnp.inf)
            s_ref[span] = s
            top = jnp.maximum(top, jnp.max(s.reshape(rows // 8, 8, cols), axis=0))
        top_ref[...] = jnp.max(top, axis=0, keepdims=True)

    def raise_scores(group):
        top = top_ref[...]
        gt = pick(gt_all, group)
        total = jnp.zeros((8, cols), f32)
        for first in range(0, blocks, SPANS):
            wide = slice(first * rows, (first + SPANS) * rows)
            dp_ref[wide] = jnp.dot(
                kv_all[2 * group + 1, wide], gt, preferred_element_type=f32
            )
            for block in range(first, first + SPANS):
                span = slice(block * rows, (block + 1) * rows)
                p = jnp.exp2((s_ref[span] - top) * log_scale)
                total = total + jnp.sum(p.reshape(rows // 8, 8, cols), axis=0)
                p_ref[span] = p.astype(bf16)
        inv_ref[...] = 1.0 / jnp.sum(total, axis=0, keepdims=True)

    def attend(group):
        inv = inv_ref[...]
        ot = jnp.dot(vt_ref[...], p_ref[...], preferred_element_type=f32) * inv
        ot = ot.astype(bf16).astype(f32)
        put(q32, group, ot)
        gt = pick(gt_all, group).astype(f32)
        delta_ref[...] = jnp.sum(gt * ot, axis=0, keepdims=True)
        gs_ref[...] = (gt * inv).astype(bf16)
        qs_ref[...] = (pick(qt_all, group).astype(f32) * inv).astype(bf16)

    def grad_scores():
        delta = delta_ref[...]
        for block in range(blocks):
            span = slice(block * rows, (block + 1) * rows)
            ds_ref[span] = (p_ref[span].astype(f32) * (dp_ref[span] - delta)).astype(bf16)

    def to_queries(group):
        dqt = jnp.dot(kt_ref[...], ds_ref[...], preferred_element_type=f32)
        put(g32, group, dqt * (inv_ref[...] * scale))

    def to_keys(unit, left, right):
        part = lax.dot_general(
            left[...], right[...], (((1,), (1,)), ((), ())), preferred_element_type=f32
        )
        for block in range(blocks):
            span = slice(block * rows, (block + 1) * rows)
            distance = blocks - 1 - block
            if distance % 2 == 0:
                part_own[unit, distance // 2] = part[span]
            else:
                part_sib[unit, distance // 2] = part[span].astype(bf16)

    lag = FIRST // 2
    prep_steps = heads // (2 * PIECES)

    def half(step, which, group):
        run = (group >= 0) & (group < groups)
        unit = 2 * group + which
        kv_event(step, 0)
        if which == 0:
            @pl.when(step == 0)
            def _():
                loads[3].wait()
                loads[4].wait()
                widen(q16, q32)
                widen(g16, g32)

            @pl.when(run)
            def _():
                @pl.when(unit == 0)
                def _():
                    for slot in range(BACK):
                        doc_share(core + slot).wait_recv()
                    find_starts()

                for slot in range(BACK):
                    kv_share(unit, core + slot).wait_recv()
                kt_ref[...] = kv_all[unit].T

        for piece in range(PIECES):
            for k in range(1, LINE):
                if KV_AT[k] % PIECES == piece:
                    kv_event(step, k)
            for j in range(BACK, -1, -1):
                if SUM_AT[j] % PIECES == piece:
                    sum_event(step, which, j)

            @pl.when(step < prep_steps)
            def _():
                prepare(step * PIECES + piece)

            @pl.when(run)
            def _():
                if which == 0:
                    if piece == 0:
                        score(group)
                    elif piece == 1:
                        for slot in range(BACK):
                            kv_share(unit + 1, core + slot).wait_recv()
                        raise_scores(group)
                    elif piece == 2:
                        vt_ref[...] = kv_all[unit + 1].T
                        attend(group)
                    else:
                        to_keys(unit, p_ref, gs_ref)
                else:
                    if piece == 0:
                        grad_scores()
                    elif piece == 1:
                        to_queries(group)
                    elif piece == 2:
                        to_keys(unit, ds_ref, qs_ref)

        @pl.when(run)
        def _():
            part_share(unit).start()

        @pl.when(group == groups)
        def _():
            if which == 0:
                by_row(q32, q16)
                pltpu.make_async_copy(q16, o_hbm, local_sems.at[0]).start()
            else:
                by_row(g32, g16)
                pltpu.make_async_copy(g16, dq_hbm, local_sems.at[1]).start()

    def body(turn, carry):
        half(2 * turn, 0, turn - lag)
        half(2 * turn + 1, 1, turn - lag)
        return carry

    steps = units + FIRST + 1 + max(SUM_AT) // PIECES
    lax.fori_loop(0, -(-steps // 2), body, 0)

    k16[...] = k32[...].astype(bf16)
    v16[...] = v32[...].astype(bf16)
    stores = [
        pltpu.make_async_copy(q16, o_hbm, local_sems.at[0]),
        pltpu.make_async_copy(g16, dq_hbm, local_sems.at[1]),
        pltpu.make_async_copy(k16, dk_hbm, local_sems.at[2]),
        pltpu.make_async_copy(v16, dv_hbm, local_sems.at[3]),
    ]
    stores[2].start()
    stores[3].start()

    def drain(ref, index):
        pltpu.make_async_copy(ref, ref, send_sems.at[index]).wait()

    moved = pl.ds(rows, BACK * rows)
    drain(kv_all.at[:, moved], 0)
    drain(kv_all.at[:, moved], 1)
    drain(doc_all.at[pl.ds(0, 8 * BACK)], 2)
    drain(doc_all.at[pl.ds(0, 8 * BACK)], 3)
    drain(part_sib, 4)
    drain(sums, 5)
    for store in stores:
        store.wait()


def settle(*refs):
    count = len(refs) // 2
    for index in range(count):
        refs[count + index][...] = refs[index][...]


def shards(queries, keys, values, grad_out, doc_ids):
    rows, heads, head = queries.shape
    groups = keys.shape[1]
    members = heads // groups
    units = 2 * groups
    cols = members * rows
    blocks = 2 * BACK + 1
    window = blocks * rows
    f32, bf16 = jnp.float32, jnp.bfloat16

    def flat(array):
        return array.reshape(-1, head)

    def by_part(shape):
        return pl.BlockSpec((shape[0] // 4, head), lambda index: (index, 0))

    anywhere = pl.BlockSpec(memory_space=pl.ANY)
    DMA = pltpu.SemaphoreType.DMA
    big, small = (heads * rows, head), (groups * rows, head)
    shapes = [jax.ShapeDtypeStruct(shape, bf16) for shape in (big, big, small, small)]
    results = pl.pallas_call(
        kernel,
        out_shape=shapes,
        in_specs=[anywhere] * 5,
        out_specs=[anywhere] * 4,
        scratch_shapes=[
            pltpu.VMEM(big, bf16),
            pltpu.VMEM(big, bf16),
            pltpu.VMEM(small, bf16),
            pltpu.VMEM(small, bf16),
            pltpu.VMEM((1, rows), jnp.int32),
            pltpu.VMEM(big, f32),
            pltpu.VMEM(big, f32),
            pltpu.VMEM(small, f32),
            pltpu.VMEM(small, f32),
            pltpu.VMEM((heads, head, rows), bf16),
            pltpu.VMEM((heads, head, rows), bf16),
            pltpu.VMEM((units, window, head), bf16),
            pltpu.VMEM((8 * blocks, rows), jnp.int32),
            pltpu.VMEM((units, LINE, rows, head), f32),
            pltpu.VMEM((units, BACK, rows, head), bf16),
            pltpu.VMEM((units, LINE, rows, head), bf16),
            pltpu.VMEM((units, BACK, rows, head), bf16),
            pltpu.VMEM((units, BACK, rows, head), bf16),
            pltpu.VMEM((window, cols), f32),
            pltpu.VMEM((window, cols), f32),
            pltpu.VMEM((window, cols), bf16),
            pltpu.VMEM((window, cols), bf16),
            pltpu.VMEM((head, cols), bf16),
            pltpu.VMEM((head, cols), bf16),
            pltpu.VMEM((head, window), bf16),
            pltpu.VMEM((head, window), bf16),
            pltpu.VMEM((1, cols), jnp.int32),
            pltpu.VMEM((1, cols), f32),
            pltpu.VMEM((1, cols), f32),
            pltpu.VMEM((1, cols), f32),
            DMA((units, BACK)),
            DMA((units, BACK)),
            DMA((BACK,)),
            DMA((BACK,)),
            DMA((units,)),
            DMA((units, BACK)),
            DMA((6,)),
            DMA((5,)),
        ],
        compiler_params=pltpu.CompilerParams(
            collective_id=0, has_side_effects=True, vmem_limit_bytes=60 * 1024 * 1024
        ),
        name="ring_attention",
    )(flat(queries), flat(grad_out), flat(keys), flat(values), doc_ids.reshape(1, rows))
    out, dq, dk, dv = pl.pallas_call(
        settle,
        out_shape=shapes,
        grid=(4,),
        in_specs=[by_part(shape) for shape in (big, big, small, small)],
        out_specs=[by_part(shape) for shape in (big, big, small, small)],
        name="settle",
    )(*results)
    return (
        out.reshape(rows, heads, head), dq.reshape(rows, heads, head),
        dk.reshape(rows, groups, head), dv.reshape(rows, groups, head),
    )


def solution(mesh):
    spec = P(("dp", "seq"), None, None)
    return jax.shard_map(
        shards,
        mesh=mesh,
        in_specs=(spec, spec, spec, spec, P(("dp", "seq"))),
        out_specs=(spec, spec, spec, spec),
        check_vma=False,
    )
```

```python
import functools
import math

import jax
import jax.numpy as jnp
from jax import lax
from jax.experimental import pallas as pl
from jax.experimental.pallas import tpu as pltpu
from jax.sharding import PartitionSpec as P

MESH = pl.DeviceIdType.MESH
BACK = 4
LINE = BACK + 1
PIECES = 4
SPANS = 3
FIRST = 6
KV_AT = (-5, 1, 7, 13, 19)
SUM_AT = (22, 17, 12, 7, 2)
SUM_LATE = (12, 3, 7, 2, 2)
LATE = 2
DOC_VALUES = 6


def rows_at(distance, rows):
    return pl.ds(pl.multiple_of((2 * BACK - distance) * rows, rows), rows)


def kernel(
    q_hbm, g_hbm, k_hbm, v_hbm, doc_hbm, o_hbm, dq_hbm, dk_hbm, dv_hbm,
    q16, g16, k16, v16, doc_row, q32, g32, k32, v32, qt_all, gt_all,
    kv_all, doc_all, part_own, part_sib, sib_got, sums, sums_got,
    s_ref, dp_ref, p_ref, ds_ref, qs_ref, gs_ref, kt_ref, vt_ref,
    start_ref, top_ref, delta_ref, inv_ref,
    kv_up_recv, kv_sib_recv, doc_up_recv, doc_sib_recv, sib_recv, sums_recv,
    send_sems, local_sems,
):
    units, window, head = kv_all.shape
    rows = doc_row.shape[1]
    groups = units // 2
    cols = s_ref.shape[1]
    members = cols // rows
    heads = members * groups
    blocks = window // rows
    size = lax.axis_size("seq")
    me = lax.axis_index("seq")
    core = lax.rem(me, 2)
    up = lax.rem(me + 2, size)
    down = lax.rem(me + size - 2, size)
    up2 = lax.rem(me + 4, size)
    down2 = lax.rem(me + size - 4, size)
    sib = me + 1 - 2 * core
    scale = 1.0 / math.sqrt(head)
    log_scale = scale * math.log2(math.e)
    f32, bf16 = jnp.float32, jnp.bfloat16

    barrier = pltpu.get_barrier_semaphore()
    for other in (up, down, up2, down2, sib):
        pl.semaphore_signal(barrier, inc=1, device_id={"seq": other}, device_id_type=MESH)

    loads = [
        pltpu.make_async_copy(src, dst, local_sems.at[index])
        for index, (src, dst) in enumerate(
            ((k_hbm, k16), (v_hbm, v16), (doc_hbm, doc_row), (q_hbm, q16), (g_hbm, g16))
        )
    ]
    for load in loads:
        load.start()
    sib_got[:, 0] = jnp.zeros((units, rows, head), bf16)
    sib_got[:, BACK] = jnp.zeros((units, rows, head), bf16)
    for load in loads[:3]:
        load.wait()
    k32[...] = k16[...].astype(f32)
    v32[...] = v16[...].astype(f32)
    own = slice(window - rows, window)
    for group in range(groups):
        kv_all[2 * group, own, :] = k32[pl.ds(group, rows, stride=groups), :].astype(bf16)
        kv_all[2 * group + 1, own, :] = v32[pl.ds(group, rows, stride=groups), :].astype(bf16)
    doc_all[16 * BACK : 16 * BACK + 8, :] = jnp.broadcast_to(doc_row[...], (8, rows))
    pl.semaphore_wait(barrier, 5)

    def remote(src, dst, send, recv, to):
        return pltpu.make_async_remote_copy(
            src_ref=src, dst_ref=dst, send_sem=send_sems.at[send], recv_sem=recv,
            device_id={"seq": to}, device_id_type=MESH,
        )

    def kv_up(unit, k):
        return remote(
            kv_all.at[unit, rows_at(2 * k, rows)], kv_all.at[unit, rows_at(2 * k + 2, rows)],
            0, kv_up_recv.at[unit, k], up,
        )

    def kv_share(unit, k):
        slot = k - core
        return remote(
            kv_all.at[unit, rows_at(2 * k, rows)], kv_all.at[unit, rows_at(2 * slot + 1, rows)],
            1, kv_sib_recv.at[unit, slot], sib,
        )

    def doc_up(k):
        return remote(
            doc_all.at[rows_at(2 * k, 8)], doc_all.at[rows_at(2 * k + 2, 8)],
            2, doc_up_recv.at[k], up,
        )

    def doc_share(k):
        slot = k - core
        return remote(
            doc_all.at[rows_at(2 * k, 8)], doc_all.at[rows_at(2 * slot + 1, 8)],
            3, doc_sib_recv.at[slot], sib,
        )

    def part_share(unit):
        return remote(
            part_sib.at[unit], sib_got.at[unit, pl.ds(1 - core, BACK)],
            4, sib_recv.at[unit], sib,
        )

    def sum_down(unit, j, hops):
        return remote(
            sums.at[unit, j - 1], sums_got.at[unit, j - 1],
            5, sums_recv.at[unit, j - 1], down if hops == 1 else down2,
        )

    def kv_event(unit, k):
        with_docs = isinstance(unit, int) and unit == 0
        if k > 0:
            if with_docs:
                doc_up(k - 1).wait_recv()
            kv_up(unit, k - 1).wait_recv()
        if k < BACK:
            if with_docs:
                doc_up(k).start()
            kv_up(unit, k).start()

        def share():
            if with_docs:
                doc_share(k).start()
            kv_share(unit, k).start()

        if k == 0:
            pl.when(core == 0)(share)
        elif k == BACK:
            pl.when(core == 1)(share)
        else:
            share()

    def sum_event(unit, kind, j, late):
        if j == BACK:
            part_share(unit).wait_recv()
        total = part_own[unit, j] + sib_got[unit, j].astype(f32)
        if late:
            sources, hops = {2: (2, 3), 0: (0, 1)}.get(j, ()), 2 - j % 2
        else:
            sources, hops = (j,) if j < BACK else (), 1
        for source in sources:
            sum_down(unit, source + 1, 1).wait_recv()
            total = total + sums_got[unit, source].astype(f32)
        if j > 0:
            sums[unit, j - 1] = total.astype(bf16)
            sum_down(unit, j, hops).start()
        elif kind == 1:
            k32[pl.ds(unit // 2, rows, stride=groups), :] = total * scale
        else:
            v32[pl.ds(unit // 2, rows, stride=groups), :] = total

    def find_starts():
        docs = doc_row[...]
        old = lax.broadcasted_iota(jnp.int32, (8 * blocks, rows), 0) // 8
        old = old + (me - 2 * BACK) < 0
        all_docs = jnp.where(old, -1, doc_all[...])
        start = jnp.zeros((1, rows), jnp.int32)
        for value in range(DOC_VALUES):
            less = jnp.where(all_docs < value, 1, 0)
            count = jnp.sum(jnp.sum(less, axis=0, keepdims=True), axis=1, keepdims=True) // 8
            start = jnp.where(docs == value, count, start)
        for member in range(members):
            start_ref[:, member * rows : (member + 1) * rows] = start

    def widen(source, dest):
        def move(index, carry):
            at = pl.ds(pl.multiple_of(index * 256, 256), 256)
            dest[at, :] = source[at, :].astype(dest.dtype)
            return carry

        lax.fori_loop(0, source.shape[0] // 256, move, 0)

    def by_row(source, dest):
        def move(index, carry):
            pair = [
                source[pl.ds(2 * index + odd, heads, stride=rows), :] for odd in (0, 1)
            ]
            at = pl.ds(pl.multiple_of(2 * heads * index, 2 * heads), 2 * heads)
            dest[at, :] = jnp.concatenate(pair, axis=0).astype(dest.dtype)
            return carry

        lax.fori_loop(0, rows // 2, move, 0)

    def prepare(number):
        for index in range(min(3 * number, heads), min(3 * number + 3, heads)):
            every = pl.ds(index, rows, stride=heads)
            qt_all[index] = q32[every, :].T.astype(bf16)
            gt_all[index] = g32[every, :].T.astype(bf16)

    def pick(ref, group):
        return jnp.concatenate([ref[group * members + index] for index in range(members)], axis=1)

    def put(ref, group, value):
        for index in range(members):
            at = pl.ds(pl.multiple_of((group * members + index) * rows, rows), rows)
            ref[at, :] = value[:, index * rows : (index + 1) * rows].T

    def score(group):
        start = start_ref[...]
        s_ref[...] = jnp.dot(kv_all[2 * group], pick(qt_all, group), preferred_element_type=f32)
        top = jnp.full((8, cols), -jnp.inf, f32)
        for block in range(blocks):
            span = slice(block * rows, (block + 1) * rows)
            where = block * rows + lax.broadcasted_iota(jnp.int32, (rows, cols), 0)
            allowed = where >= start
            if block == blocks - 1:
                mine = lax.broadcasted_iota(jnp.int32, (rows, cols), 1) % rows
                allowed = allowed & (where - block * rows <= mine)
            s = jnp.where(allowed, s_ref[span], -jnp.inf)
            s_ref[span] = s
            top = jnp.maximum(top, jnp.max(s.reshape(rows // 8, 8, cols), axis=0))
        top_ref[...] = jnp.max(top, axis=0, keepdims=True)

    def raise_scores(group):
        top = top_ref[...]
        gt = pick(gt_all, group)
        total = jnp.zeros((8, cols), f32)
        for first in range(0, blocks, SPANS):
            wide = slice(first * rows, (first + SPANS) * rows)
            dp_ref[wide] = jnp.dot(
                kv_all[2 * group + 1, wide], gt, preferred_element_type=f32
            )
            for block in range(first, first + SPANS):
                span = slice(block * rows, (block + 1) * rows)
                p = jnp.exp2((s_ref[span] - top) * log_scale)
                total = total + jnp.sum(p.reshape(rows // 8, 8, cols), axis=0)
                p_ref[span] = p.astype(bf16)
        inv_ref[...] = 1.0 / jnp.sum(total, axis=0, keepdims=True)

    def attend(group):
        inv = inv_ref[...]
        ot = jnp.dot(vt_ref[...], p_ref[...], preferred_element_type=f32) * inv
        ot = ot.astype(bf16).astype(f32)
        put(q32, group, ot)
        gt = pick(gt_all, group).astype(f32)
        delta_ref[...] = jnp.sum(gt * ot, axis=0, keepdims=True)
        gs_ref[...] = (gt * inv).astype(bf16)
        qs_ref[...] = (pick(qt_all, group).astype(f32) * inv).astype(bf16)

    def grad_scores():
        delta = delta_ref[...]
        for block in range(blocks):
            span = slice(block * rows, (block + 1) * rows)
            ds_ref[span] = (p_ref[span].astype(f32) * (dp_ref[span] - delta)).astype(bf16)

    def to_queries(group):
        dqt = jnp.dot(kt_ref[...], ds_ref[...], preferred_element_type=f32)
        put(g32, group, dqt * (inv_ref[...] * scale))

    def to_keys(unit, left, right):
        part = lax.dot_general(
            left[...], right[...], (((1,), (1,)), ((), ())), preferred_element_type=f32
        )
        for block in range(blocks):
            span = slice(block * rows, (block + 1) * rows)
            distance = blocks - 1 - block
            if distance % 2 == 0:
                part_own[unit, distance // 2] = part[span]
            else:
                part_sib[unit, distance // 2] = part[span].astype(bf16)

    begin, end = PIECES * FIRST, PIECES * (FIRST + units)
    before = {}
    for unit in range(units):
        for k in range(LINE):
            when = PIECES * unit + KV_AT[k]
            if when < begin:
                before.setdefault(max(when, 0), []).append((unit, k))
    for now in range(begin):
        for unit, k in before.get(now, ()):
            kv_event(unit, k)
        if now == 0:
            loads[3].wait()
            loads[4].wait()
            widen(q16, q32)
            widen(g16, g32)
        prepare(now)
    for slot in range(BACK):
        doc_share(core + slot).wait_recv()
    find_starts()

    def half(step, which, group):
        for piece in range(PIECES):
            for k in range(LINE):
                unit = step - KV_AT[k] // PIECES
                if KV_AT[k] % PIECES == piece:
                    @pl.when(unit < units)
                    def _():
                        kv_event(unit, k)

            for j in range(BACK, -1, -1):
                for late, table in enumerate((SUM_AT, SUM_LATE)):
                    back = FIRST + 1 + table[j] // PIECES
                    if table[j] % PIECES != piece or table[j] > PIECES and late:
                        continue
                    unit = step - back
                    if late:
                        live = (unit >= units - LATE) & (unit < units)
                    else:
                        live = (unit >= 0) & (unit < units - LATE)

                    @pl.when(live)
                    def _():
                        sum_event(unit, (which - back) % 2, j, late == 1)

            unit = 2 * group + which

            @pl.when(me >= 0)
            def _():
                if which == 0:
                    if piece == 0:
                        for slot in range(BACK):
                            kv_share(unit, core + slot).wait_recv()
                        score(group)
                    elif piece == 1:
                        for slot in range(BACK):
                            kv_share(unit + 1, core + slot).wait_recv()
                        raise_scores(group)
                    elif piece == 2:
                        vt_ref[...] = kv_all[unit + 1].T
                        attend(group)
                    else:
                        to_keys(unit, p_ref, gs_ref)
                else:
                    if piece == 0:
                        grad_scores()
                        kt_ref[...] = kv_all[unit - 1].T
                    elif piece == 1:
                        to_queries(group)
                    elif piece == 2:
                        to_keys(unit, ds_ref, qs_ref)
        part_share(unit).start()

    def body(group, carry):
        half(2 * group + FIRST, 0, group)
        half(2 * group + FIRST + 1, 1, group)
        return carry

    lax.fori_loop(0, groups, body, 0)

    after = {}
    for unit in range(units):
        late = unit >= units - LATE
        table = SUM_LATE if late else SUM_AT
        for j in range(BACK, -1, -1):
            when = PIECES * (FIRST + 1 + unit) + table[j]
            if when >= end or late and table[j] > PIECES:
                after.setdefault(when, []).append((unit, j))
    moves = [(q32, q16, o_hbm, 0), (g32, g16, dq_hbm, 1)]
    for now in sorted(after):
        for unit, j in after[now]:
            sum_event(unit, unit % 2, j, unit >= units - LATE)
        if moves and now >= end + 2:
            wide, narrow, result, index = moves.pop(0)
            by_row(wide, narrow)
            pltpu.make_async_copy(narrow, result, local_sems.at[index]).start()

    k16[...] = k32[...].astype(bf16)
    v16[...] = v32[...].astype(bf16)
    stores = [
        pltpu.make_async_copy(q16, o_hbm, local_sems.at[0]),
        pltpu.make_async_copy(g16, dq_hbm, local_sems.at[1]),
        pltpu.make_async_copy(k16, dk_hbm, local_sems.at[2]),
        pltpu.make_async_copy(v16, dv_hbm, local_sems.at[3]),
    ]
    stores[2].start()
    stores[3].start()

    def drain(ref, index):
        pltpu.make_async_copy(ref, ref, send_sems.at[index]).wait()

    moved = pl.ds(rows, BACK * rows)
    drain(kv_all.at[:, moved], 0)
    drain(kv_all.at[:, moved], 1)
    drain(doc_all.at[pl.ds(0, 8 * BACK)], 2)
    drain(doc_all.at[pl.ds(0, 8 * BACK)], 3)
    drain(part_sib, 4)
    drain(sums, 5)
    for store in stores:
        store.wait()


def settle(*refs):
    count = 4
    sources, results, held = refs[:count], refs[count : 2 * count], refs[2 * count : 3 * count]
    sems = refs[-1]
    pairs = []
    for index in range(count):
        size = held[index].shape[0]
        part = min(size, 1280)
        for first in range(0, size, part):
            at = pl.ds(first, part)
            inward = pltpu.make_async_copy(
                sources[index].at[at], held[index].at[at], sems.at[0, len(pairs)]
            )
            outward = pltpu.make_async_copy(
                held[index].at[at], results[index].at[at], sems.at[1, len(pairs)]
            )
            pairs.append((inward, outward))
    for inward, outward in pairs:
        inward.start()
    for inward, outward in pairs:
        inward.wait()
        outward.start()
    for inward, outward in pairs:
        outward.wait()


def shards(queries, keys, values, grad_out, doc_ids):
    rows, heads, head = queries.shape
    groups = keys.shape[1]
    members = heads // groups
    units = 2 * groups
    cols = members * rows
    blocks = 2 * BACK + 1
    window = blocks * rows
    f32, bf16 = jnp.float32, jnp.bfloat16

    def flat(array):
        return array.reshape(-1, head)

    anywhere = pl.BlockSpec(memory_space=pl.ANY)
    DMA = pltpu.SemaphoreType.DMA
    big, small = (heads * rows, head), (groups * rows, head)
    shapes = [jax.ShapeDtypeStruct(shape, bf16) for shape in (big, big, small, small)]
    results = pl.pallas_call(
        kernel,
        out_shape=shapes,
        in_specs=[anywhere] * 5,
        out_specs=[anywhere] * 4,
        scratch_shapes=[
            pltpu.VMEM(big, bf16),
            pltpu.VMEM(big, bf16),
            pltpu.VMEM(small, bf16),
            pltpu.VMEM(small, bf16),
            pltpu.VMEM((1, rows), jnp.int32),
            pltpu.VMEM(big, f32),
            pltpu.VMEM(big, f32),
            pltpu.VMEM(small, f32),
            pltpu.VMEM(small, f32),
            pltpu.VMEM((heads, head, rows), bf16),
            pltpu.VMEM((heads, head, rows), bf16),
            pltpu.VMEM((units, window, head), bf16),
            pltpu.VMEM((8 * blocks, rows), jnp.int32),
            pltpu.VMEM((units, LINE, rows, head), f32),
            pltpu.VMEM((units, BACK, rows, head), bf16),
            pltpu.VMEM((units, LINE, rows, head), bf16),
            pltpu.VMEM((units, BACK, rows, head), bf16),
            pltpu.VMEM((units, BACK, rows, head), bf16),
            pltpu.VMEM((window, cols), f32),
            pltpu.VMEM((window, cols), f32),
            pltpu.VMEM((window, cols), bf16),
            pltpu.VMEM((window, cols), bf16),
            pltpu.VMEM((head, cols), bf16),
            pltpu.VMEM((head, cols), bf16),
            pltpu.VMEM((head, window), bf16),
            pltpu.VMEM((head, window), bf16),
            pltpu.VMEM((1, cols), jnp.int32),
            pltpu.VMEM((1, cols), f32),
            pltpu.VMEM((1, cols), f32),
            pltpu.VMEM((1, cols), f32),
            DMA((units, BACK)),
            DMA((units, BACK)),
            DMA((BACK,)),
            DMA((BACK,)),
            DMA((units,)),
            DMA((units, BACK)),
            DMA((6,)),
            DMA((5,)),
        ],
        compiler_params=pltpu.CompilerParams(
            collective_id=0, has_side_effects=True, vmem_limit_bytes=60 * 1024 * 1024
        ),
        name="ring_attention",
    )(flat(queries), flat(grad_out), flat(keys), flat(values), doc_ids.reshape(1, rows))
    out, dq, dk, dv = pl.pallas_call(
        settle,
        out_shape=shapes,
        in_specs=[anywhere] * 4,
        out_specs=[anywhere] * 4,
        scratch_shapes=[pltpu.VMEM(shape, bf16) for shape in (big, big, small, small)]
        + [DMA((2, 10))],
        name="settle",
    )(*results)
    return (
        out.reshape(rows, heads, head), dq.reshape(rows, heads, head),
        dk.reshape(rows, groups, head), dv.reshape(rows, groups, head),
    )


def solution(mesh):
    spec = P(("dp", "seq"), None, None)
    return jax.shard_map(
        shards,
        mesh=mesh,
        in_specs=(spec, spec, spec, spec, P(("dp", "seq"))),
        out_specs=(spec, spec, spec, spec),
        check_vma=False,
    )
```

```python
import functools
import math

import jax
import jax.numpy as jnp
from jax import lax
from jax.experimental import pallas as pl
from jax.experimental.pallas import tpu as pltpu
from jax.sharding import PartitionSpec as P

MESH = pl.DeviceIdType.MESH
BACK = 4
LINE = BACK + 1
PIECES = 4
SPANS = 3
FIRST = 6
KV_AT = (-5, 1, 7, 13, 19)
SUM_AT = (22, 17, 12, 7, 2)
SUM_LATE = (12, 3, 7, 2, 2)
LATE = 2
DOC_VALUES = 6


def rows_at(distance, rows):
    return pl.ds(pl.multiple_of((2 * BACK - distance) * rows, rows), rows)


def kernel(
    q_hbm, g_hbm, k_hbm, v_hbm, doc_hbm, o_hbm, dq_hbm, dk_hbm, dv_hbm,
    q16, g16, k16, v16, doc_row, q32, g32, k32, v32, qt_all, gt_all,
    kv_all, doc_all, part_own, part_sib, sib_got, sums, sums_got,
    s_ref, dp_ref, p_ref, ds_ref, qs_ref, gs_ref, kt_ref, vt_ref,
    start_ref, top_ref, delta_ref, inv_ref,
    kv_up_recv, kv_sib_recv, doc_up_recv, doc_sib_recv, sib_recv, sums_recv,
    send_sems, local_sems,
):
    units, window, head = kv_all.shape
    rows = doc_row.shape[1]
    groups = units // 2
    cols = s_ref.shape[1]
    members = cols // rows
    heads = members * groups
    blocks = window // rows
    size = lax.axis_size("seq")
    me = lax.axis_index("seq")
    core = lax.rem(me, 2)
    up = lax.rem(me + 2, size)
    down = lax.rem(me + size - 2, size)
    up2 = lax.rem(me + 4, size)
    down2 = lax.rem(me + size - 4, size)
    sib = me + 1 - 2 * core
    scale = 1.0 / math.sqrt(head)
    log_scale = scale * math.log2(math.e)
    f32, bf16 = jnp.float32, jnp.bfloat16

    barrier = pltpu.get_barrier_semaphore()
    for other in (up, down, up2, down2, sib):
        pl.semaphore_signal(barrier, inc=1, device_id={"seq": other}, device_id_type=MESH)

    loads = [
        pltpu.make_async_copy(src, dst, local_sems.at[index])
        for index, (src, dst) in enumerate(
            ((k_hbm, k16), (v_hbm, v16), (doc_hbm, doc_row), (q_hbm, q16), (g_hbm, g16))
        )
    ]
    for load in loads:
        load.start()
    sib_got[:, 0] = jnp.zeros((units, rows, head), bf16)
    sib_got[:, BACK] = jnp.zeros((units, rows, head), bf16)
    for load in loads[:3]:
        load.wait()
    k32[...] = k16[...].astype(f32)
    v32[...] = v16[...].astype(f32)
    own = slice(window - rows, window)
    for group in range(groups):
        kv_all[2 * group, own, :] = k32[pl.ds(group, rows, stride=groups), :].astype(bf16)
        kv_all[2 * group + 1, own, :] = v32[pl.ds(group, rows, stride=groups), :].astype(bf16)
    doc_all[16 * BACK : 16 * BACK + 8, :] = jnp.broadcast_to(doc_row[...], (8, rows))
    pl.semaphore_wait(barrier, 5)

    def remote(src, dst, send, recv, to):
        return pltpu.make_async_remote_copy(
            src_ref=src, dst_ref=dst, send_sem=send_sems.at[send], recv_sem=recv,
            device_id={"seq": to}, device_id_type=MESH,
        )

    def kv_up(unit, k):
        return remote(
            kv_all.at[unit, rows_at(2 * k, rows)], kv_all.at[unit, rows_at(2 * k + 2, rows)],
            0, kv_up_recv.at[unit, k], up,
        )

    def kv_share(unit, k):
        slot = k - core
        return remote(
            kv_all.at[unit, rows_at(2 * k, rows)], kv_all.at[unit, rows_at(2 * slot + 1, rows)],
            1, kv_sib_recv.at[unit, slot], sib,
        )

    def doc_up(k):
        return remote(
            doc_all.at[rows_at(2 * k, 8)], doc_all.at[rows_at(2 * k + 2, 8)],
            2, doc_up_recv.at[k], up,
        )

    def doc_share(k):
        slot = k - core
        return remote(
            doc_all.at[rows_at(2 * k, 8)], doc_all.at[rows_at(2 * slot + 1, 8)],
            3, doc_sib_recv.at[slot], sib,
        )

    def part_share(unit):
        return remote(
            part_sib.at[unit], sib_got.at[unit, pl.ds(1 - core, BACK)],
            4, sib_recv.at[unit], sib,
        )

    def sum_down(unit, j, hops):
        return remote(
            sums.at[unit, j - 1], sums_got.at[unit, j - 1],
            5, sums_recv.at[unit, j - 1], down if hops == 1 else down2,
        )

    def kv_event(unit, k):
        with_docs = isinstance(unit, int) and unit == 0
        if k > 0:
            if with_docs:
                doc_up(k - 1).wait_recv()
            kv_up(unit, k - 1).wait_recv()
        if k < BACK:
            if with_docs:
                doc_up(k).start()
            kv_up(unit, k).start()

        def share():
            if with_docs:
                doc_share(k).start()
            kv_share(unit, k).start()

        if k == 0:
            pl.when(core == 0)(share)
        elif k == BACK:
            pl.when(core == 1)(share)
        else:
            share()

    def sum_event(unit, kind, j, late):
        if j == BACK:
            part_share(unit).wait_recv()
        total = part_own[unit, j] + sib_got[unit, j].astype(f32)
        if late:
            sources, hops = {2: (2, 3), 0: (0, 1)}.get(j, ()), 2 - j % 2
        else:
            sources, hops = (j,) if j < BACK else (), 1
        for source in sources:
            sum_down(unit, source + 1, 1).wait_recv()
            total = total + sums_got[unit, source].astype(f32)
        if j > 0:
            sums[unit, j - 1] = total.astype(bf16)
            sum_down(unit, j, hops).start()
        elif kind == 1:
            k32[pl.ds(unit // 2, rows, stride=groups), :] = total * scale
        else:
            v32[pl.ds(unit // 2, rows, stride=groups), :] = total

    def find_starts():
        docs = doc_row[...]
        old = lax.broadcasted_iota(jnp.int32, (8 * blocks, rows), 0) // 8
        old = old + (me - 2 * BACK) < 0
        all_docs = jnp.where(old, -1, doc_all[...])
        start = jnp.zeros((1, rows), jnp.int32)
        for value in range(DOC_VALUES):
            less = jnp.where(all_docs < value, 1, 0)
            count = jnp.sum(jnp.sum(less, axis=0, keepdims=True), axis=1, keepdims=True) // 8
            start = jnp.where(docs == value, count, start)
        for member in range(members):
            start_ref[:, member * rows : (member + 1) * rows] = start

    def widen(source, dest):
        def move(index, carry):
            at = pl.ds(pl.multiple_of(index * 256, 256), 256)
            dest[at, :] = source[at, :].astype(dest.dtype)
            return carry

        lax.fori_loop(0, source.shape[0] // 256, move, 0)

    def by_row(source, dest):
        def move(index, carry):
            pair = [
                source[pl.ds(2 * index + odd, heads, stride=rows), :] for odd in (0, 1)
            ]
            at = pl.ds(pl.multiple_of(2 * heads * index, 2 * heads), 2 * heads)
            dest[at, :] = jnp.concatenate(pair, axis=0).astype(dest.dtype)
            return carry

        lax.fori_loop(0, rows // 2, move, 0)

    def prepare(number):
        for index in range(min(3 * number, heads), min(3 * number + 3, heads)):
            every = pl.ds(index, rows, stride=heads)
            qt_all[index] = q32[every, :].T.astype(bf16)
            gt_all[index] = g32[every, :].T.astype(bf16)

    def pick(ref, group):
        return jnp.concatenate([ref[group * members + index] for index in range(members)], axis=1)

    def put(ref, group, value):
        for index in range(members):
            at = pl.ds(pl.multiple_of((group * members + index) * rows, rows), rows)
            ref[at, :] = value[:, index * rows : (index + 1) * rows].T

    def score(group):
        start = start_ref[...]
        s_ref[...] = jnp.dot(kv_all[2 * group], pick(qt_all, group), preferred_element_type=f32)
        top = jnp.full((8, cols), -jnp.inf, f32)
        for block in range(blocks):
            span = slice(block * rows, (block + 1) * rows)
            where = block * rows + lax.broadcasted_iota(jnp.int32, (rows, cols), 0)
            allowed = where >= start
            if block == blocks - 1:
                mine = lax.broadcasted_iota(jnp.int32, (rows, cols), 1) % rows
                allowed = allowed & (where - block * rows <= mine)
            s = jnp.where(allowed, s_ref[span], -jnp.inf)
            s_ref[span] = s
            top = jnp.maximum(top, jnp.max(s.reshape(rows // 8, 8, cols), axis=0))
        top_ref[...] = jnp.max(top, axis=0, keepdims=True)

    def raise_scores(group):
        top = top_ref[...]
        gt = pick(gt_all, group)
        total = jnp.zeros((8, cols), f32)
        for first in range(0, blocks, SPANS):
            wide = slice(first * rows, (first + SPANS) * rows)
            dp_ref[wide] = jnp.dot(
                kv_all[2 * group + 1, wide], gt, preferred_element_type=f32
            )
            for block in range(first, first + SPANS):
                span = slice(block * rows, (block + 1) * rows)
                p = jnp.exp2((s_ref[span] - top) * log_scale)
                total = total + jnp.sum(p.reshape(rows // 8, 8, cols), axis=0)
                p_ref[span] = p.astype(bf16)
        inv_ref[...] = 1.0 / jnp.sum(total, axis=0, keepdims=True)

    def attend(group):
        inv = inv_ref[...]
        ot = jnp.dot(vt_ref[...], p_ref[...], preferred_element_type=f32) * inv
        ot = ot.astype(bf16).astype(f32)
        put(q32, group, ot)
        gt = pick(gt_all, group).astype(f32)
        delta_ref[...] = jnp.sum(gt * ot, axis=0, keepdims=True)
        gs_ref[...] = (gt * inv).astype(bf16)
        qs_ref[...] = (pick(qt_all, group).astype(f32) * inv).astype(bf16)

    def grad_scores():
        delta = delta_ref[...]
        for block in range(blocks):
            span = slice(block * rows, (block + 1) * rows)
            ds_ref[span] = (p_ref[span].astype(f32) * (dp_ref[span] - delta)).astype(bf16)

    def to_queries(group):
        dqt = jnp.dot(kt_ref[...], ds_ref[...], preferred_element_type=f32)
        put(g32, group, dqt * (inv_ref[...] * scale))

    def to_keys(unit, left, right):
        part = lax.dot_general(
            left[...], right[...], (((1,), (1,)), ((), ())), preferred_element_type=f32
        )
        for block in range(blocks):
            span = slice(block * rows, (block + 1) * rows)
            distance = blocks - 1 - block
            if distance % 2 == 0:
                part_own[unit, distance // 2] = part[span]
            else:
                part_sib[unit, distance // 2] = part[span].astype(bf16)

    begin, end = PIECES * FIRST, PIECES * (FIRST + units)
    before = {}
    for unit in range(units):
        for k in range(LINE):
            when = PIECES * unit + KV_AT[k]
            if when < begin:
                before.setdefault(max(when, 0), []).append((unit, k))
    for now in range(begin):
        for unit, k in before.get(now, ()):
            kv_event(unit, k)
        if now == 0:
            loads[3].wait()
            loads[4].wait()
            widen(q16, q32)
            widen(g16, g32)
        prepare(now)
    for slot in range(BACK):
        doc_share(core + slot).wait_recv()
    find_starts()

    def half(step, which, group):
        for piece in range(PIECES):
            for k in range(LINE):
                unit = step - KV_AT[k] // PIECES
                if KV_AT[k] % PIECES == piece:
                    @pl.when(unit < units)
                    def _():
                        kv_event(unit, k)

            for j in range(BACK, -1, -1):
                for late, table in enumerate((SUM_AT, SUM_LATE)):
                    back = FIRST + 1 + table[j] // PIECES
                    if table[j] % PIECES != piece or table[j] > PIECES and late:
                        continue
                    unit = step - back
                    if late:
                        live = (unit >= units - LATE) & (unit < units)
                    else:
                        live = (unit >= 0) & (unit < units - LATE)

                    @pl.when(live)
                    def _():
                        sum_event(unit, (which - back) % 2, j, late == 1)

            unit = 2 * group + which

            @pl.when(me >= 0)
            def _():
                if which == 0:
                    if piece == 0:
                        for slot in range(BACK):
                            kv_share(unit, core + slot).wait_recv()
                        score(group)
                    elif piece == 1:
                        for slot in range(BACK):
                            kv_share(unit + 1, core + slot).wait_recv()
                        raise_scores(group)
                    elif piece == 2:
                        vt_ref[...] = kv_all[unit + 1].T
                        attend(group)
                    else:
                        to_keys(unit, p_ref, gs_ref)
                else:
                    if piece == 0:
                        grad_scores()
                        kt_ref[...] = kv_all[unit - 1].T
                    elif piece == 1:
                        to_queries(group)
                    elif piece == 2:
                        to_keys(unit, ds_ref, qs_ref)
        part_share(unit).start()

    def body(group, carry):
        half(2 * group + FIRST, 0, group)
        half(2 * group + FIRST + 1, 1, group)
        return carry

    lax.fori_loop(0, groups, body, 0)

    after = {}
    for unit in range(units):
        late = unit >= units - LATE
        table = SUM_LATE if late else SUM_AT
        for j in range(BACK, -1, -1):
            when = PIECES * (FIRST + 1 + unit) + table[j]
            if when >= end or late and table[j] > PIECES:
                after.setdefault(when, []).append((unit, j))
    moves = [(q32, q16, o_hbm, 0), (g32, g16, dq_hbm, 1)]
    values_end = max(now for now in after if any(unit % 2 == 0 for unit, j in after[now]))
    for now in sorted(after):
        for unit, j in after[now]:
            sum_event(unit, unit % 2, j, unit >= units - LATE)
        if now == values_end:
            v16[...] = v32[...].astype(bf16)
            pltpu.make_async_copy(v16, dv_hbm, local_sems.at[3]).start()
        if moves and now >= end + 2:
            wide, narrow, result, index = moves.pop(0)
            by_row(wide, narrow)
            pltpu.make_async_copy(narrow, result, local_sems.at[index]).start()

    k16[...] = k32[...].astype(bf16)
    stores = [
        pltpu.make_async_copy(q16, o_hbm, local_sems.at[0]),
        pltpu.make_async_copy(g16, dq_hbm, local_sems.at[1]),
        pltpu.make_async_copy(k16, dk_hbm, local_sems.at[2]),
        pltpu.make_async_copy(v16, dv_hbm, local_sems.at[3]),
    ]
    stores[2].start()

    def drain(ref, index):
        pltpu.make_async_copy(ref, ref, send_sems.at[index]).wait()

    moved = pl.ds(rows, BACK * rows)
    drain(kv_all.at[:, moved], 0)
    drain(kv_all.at[:, moved], 1)
    drain(doc_all.at[pl.ds(0, 8 * BACK)], 2)
    drain(doc_all.at[pl.ds(0, 8 * BACK)], 3)
    drain(part_sib, 4)
    drain(sums, 5)
    for store in stores:
        store.wait()


def settle(*refs):
    count = 4
    sources, results, held = refs[:count], refs[count : 2 * count], refs[2 * count : 3 * count]
    sems = refs[-1]
    pairs = []
    for index in range(count):
        size = held[index].shape[0]
        part = min(size, 512)
        for first in range(0, size, part):
            at = pl.ds(first, part)
            inward = pltpu.make_async_copy(
                sources[index].at[at], held[index].at[at], sems.at[0, len(pairs)]
            )
            outward = pltpu.make_async_copy(
                held[index].at[at], results[index].at[at], sems.at[1, len(pairs)]
            )
            pairs.append((inward, outward))
    for inward, outward in pairs:
        inward.start()
    for inward, outward in pairs:
        inward.wait()
        outward.start()
    for inward, outward in pairs:
        outward.wait()


def shards(queries, keys, values, grad_out, doc_ids):
    rows, heads, head = queries.shape
    groups = keys.shape[1]
    members = heads // groups
    units = 2 * groups
    cols = members * rows
    blocks = 2 * BACK + 1
    window = blocks * rows
    f32, bf16 = jnp.float32, jnp.bfloat16

    def flat(array):
        return array.reshape(-1, head)

    anywhere = pl.BlockSpec(memory_space=pl.ANY)
    DMA = pltpu.SemaphoreType.DMA
    big, small = (heads * rows, head), (groups * rows, head)
    shapes = [jax.ShapeDtypeStruct(shape, bf16) for shape in (big, big, small, small)]
    results = pl.pallas_call(
        kernel,
        out_shape=shapes,
        in_specs=[anywhere] * 5,
        out_specs=[anywhere] * 4,
        scratch_shapes=[
            pltpu.VMEM(big, bf16),
            pltpu.VMEM(big, bf16),
            pltpu.VMEM(small, bf16),
            pltpu.VMEM(small, bf16),
            pltpu.VMEM((1, rows), jnp.int32),
            pltpu.VMEM(big, f32),
            pltpu.VMEM(big, f32),
            pltpu.VMEM(small, f32),
            pltpu.VMEM(small, f32),
            pltpu.VMEM((heads, head, rows), bf16),
            pltpu.VMEM((heads, head, rows), bf16),
            pltpu.VMEM((units, window, head), bf16),
            pltpu.VMEM((8 * blocks, rows), jnp.int32),
            pltpu.VMEM((units, LINE, rows, head), f32),
            pltpu.VMEM((units, BACK, rows, head), bf16),
            pltpu.VMEM((units, LINE, rows, head), bf16),
            pltpu.VMEM((units, BACK, rows, head), bf16),
            pltpu.VMEM((units, BACK, rows, head), bf16),
            pltpu.VMEM((window, cols), f32),
            pltpu.VMEM((window, cols), f32),
            pltpu.VMEM((window, cols), bf16),
            pltpu.VMEM((window, cols), bf16),
            pltpu.VMEM((head, cols), bf16),
            pltpu.VMEM((head, cols), bf16),
            pltpu.VMEM((head, window), bf16),
            pltpu.VMEM((head, window), bf16),
            pltpu.VMEM((1, cols), jnp.int32),
            pltpu.VMEM((1, cols), f32),
            pltpu.VMEM((1, cols), f32),
            pltpu.VMEM((1, cols), f32),
            DMA((units, BACK)),
            DMA((units, BACK)),
            DMA((BACK,)),
            DMA((BACK,)),
            DMA((units,)),
            DMA((units, BACK)),
            DMA((6,)),
            DMA((5,)),
        ],
        compiler_params=pltpu.CompilerParams(
            collective_id=0, has_side_effects=True, vmem_limit_bytes=60 * 1024 * 1024
        ),
        name="ring_attention",
    )(flat(queries), flat(grad_out), flat(keys), flat(values), doc_ids.reshape(1, rows))
    out, dq, dk, dv = pl.pallas_call(
        settle,
        out_shape=shapes,
        in_specs=[anywhere] * 4,
        out_specs=[anywhere] * 4,
        scratch_shapes=[pltpu.VMEM(shape, bf16) for shape in (big, big, small, small)]
        + [DMA((2, 24))],
        name="settle",
    )(*results)
    return (
        out.reshape(rows, heads, head), dq.reshape(rows, heads, head),
        dk.reshape(rows, groups, head), dv.reshape(rows, groups, head),
    )


def solution(mesh):
    spec = P(("dp", "seq"), None, None)
    return jax.shard_map(
        shards,
        mesh=mesh,
        in_specs=(spec, spec, spec, spec, P(("dp", "seq"))),
        out_specs=(spec, spec, spec, spec),
        check_vma=False,
    )
```
